32 devices in a mesh: parts: 2 (over y), tensor: 4 (over x, core), dp: 4 (over z).
Axes of the slice: x: 2, y: 2, z: 4, core: 2. Of those that a mesh axis runs over, the one named last changes fastest.
Arguments:
- rows_in: bfloat16 [2048, 8192], P(('parts', 'tensor'), 'dp'), parts along dimension 0, may hold values from -6 to 6
- up_weight: bfloat16 [8192, 32768], P('dp', 'tensor'), may hold values from -0.0625 to 0.0625
- up_bias: float32 [32768], P('tensor'), may hold values from -3 to 3
- down_weight: bfloat16 [32768, 8192], P('tensor', 'dp'), may hold values from -0.09375 to 0.09375
- down_bias: float32 [8192], P('dp'), may hold values from -3 to 3
- active_ids: int32 [16, 4, 8], P('parts', 'tensor'), parts along dimension 0, may hold values from 0 to 255, as said below
- active_counts: int32 [16, 4], P('parts', 'tensor'), parts along dimension 0, may hold values from 1 to 8, as said below
Outputs:
- ffn_out: float32 [2048, 8192], P(('parts', 'tensor'), 'dp'), parts along dimension 0
The draws below stay inside these ranges and needn't reach their ends.
There are 2 independent parts, one for each index of `parts`. The reference program is written for one: setup_inputs(seed, part) draws one part's arguments, and reference() takes and returns one part's arrays. A program takes and returns all parts, laid end to end along the dimension named above; an argument that names none is the same for every part. Nothing has to cross between parts.
Inputs may be any that keep to these rules, and one draw needn't show every extreme that they name: active_ids[b, t, :] are 8 distinct block ids of tensor index t's own range, t * 64 up to (t+1) * 64 - 1; entries of slots that are not live are such ids too. `active_counts`: in every row block some tensor index has exactly 8 live slots.
All inputs are finite; a program needn't handle non-finite values.
Results may differ from the reference program's by a relative error of at most 0.012.
Values may be sent and summed in bfloat16 or wider, within the bound.
No kernel may reach another device: no remote copies, remote signals or barrier semaphores. Data moves between devices by JAX's collectives and lax.ppermute only.
A program may use at most 320 MiB of HBM per device.

```python
import jax
import jax.numpy as jnp
from jax import lax

D = 8192
FF = 32768
BLK = 128
MAX_ACT = 8
ROWS = 1024
N_TENSOR = 4
N_DP = 4


def shared_layout(key):
    blocks = ROWS // BLK
    shards = N_TENSOR
    per_shard = FF // BLK // N_TENSOR
    key_order, key_busy, key_high, key_low, key_forced = jax.random.split(key, 5)
    scores = jax.random.randint(key_order, (blocks, shards, per_shard), 0, 2 ** 20) * per_shard
    scores = scores + jnp.arange(per_shard, dtype=jnp.int32)[None, None, :]
    order = jnp.argsort(scores, axis=-1)[:, :, :MAX_ACT].astype(jnp.int32)
    ids = order + (jnp.arange(shards, dtype=jnp.int32) * per_shard)[None, :, None]
    busy = jax.random.randint(key_busy, (blocks, shards), 0, 4) == 0
    high = jax.random.randint(key_high, (blocks, shards), MAX_ACT // 2 + 1, MAX_ACT + 1)
    low = jax.random.randint(key_low, (blocks, shards), 1, MAX_ACT // 2 + 1)
    counts = jnp.where(busy, high, low)
    forced = jax.random.randint(key_forced, (blocks,), 0, shards)
    counts = jnp.where(jnp.arange(shards, dtype=jnp.int32)[None, :] == forced[:, None], MAX_ACT, counts)
    return (ids.astype(jnp.int32), counts.astype(jnp.int32))


def draw_active_ids(key, part):
    return shared_layout(key)[0]


def draw_active_counts(key, part):
    return shared_layout(key)[1]


def levels(rng, shape, cuts, smallest, high):
    factor_of = 1.0
    for axis_at, parts in cuts:
        draws = jax.random.uniform(jax.random.fold_in(jax.random.fold_in(rng, 6), axis_at), (parts,), jnp.float32, smallest / len(cuts), high / len(cuts))
        factor_of = factor_of * jnp.repeat(jnp.exp(draws), shape[axis_at] // parts).reshape((-1,) + (1,) * (len(shape) - 1 - axis_at))
    return factor_of


def bell_draw(own_key, extent, scale, reach, cuts=(), held_as=jnp.bfloat16):
    result = jax.random.normal(own_key, extent, jnp.float32) * scale
    if len(cuts) > 0:
        result = levels(own_key, extent, cuts, -0.22, 0.18) * result
    return jnp.clip(result, min=-reach, max=reach).astype(held_as)


def setup_inputs(seed: int = 0, part: int = 0) -> dict:
    seeds = jax.random.split(jax.random.key(seed), 8)
    part_keys = jax.random.split(jax.random.fold_in(seeds[7], part), 8)
    rows_in = bell_draw(part_keys[0], (ROWS, D), 1.0, 6.0, ((0, 4), (1, 4)))
    up_weight = bell_draw(seeds[1], (D, FF), D ** -0.5, 0.0625, ((0, 4), (1, 4)))
    up_bias = bell_draw(seeds[2], (FF,), 0.5, 3.0, ((0, 4),), jnp.float32)
    down_weight = bell_draw(seeds[3], (FF, D), (MAX_ACT * BLK * N_TENSOR) ** -0.5, 0.09375, ((0, 4), (1, 4)))
    down_bias = bell_draw(seeds[4], (D,), 0.5, 3.0, ((0, 4),), jnp.float32)
    active_ids = draw_active_ids(jax.random.fold_in(jax.random.fold_in(seeds[7], part), 71), part)
    active_counts = draw_active_counts(jax.random.fold_in(jax.random.fold_in(seeds[7], part), 71), part)
    return dict(rows_in=rows_in, up_weight=up_weight, up_bias=up_bias, down_weight=down_weight, down_bias=down_bias, active_ids=active_ids, active_counts=active_counts)


def reference(rows_in, up_weight, up_bias, down_weight, down_bias, active_ids, active_counts):
    block_count = FF // BLK
    width_part = D // N_DP
    up_blocks = up_weight.reshape(D, block_count, BLK)
    down_blocks = down_weight.reshape(block_count, BLK, D)
    bias_blocks = up_bias.reshape(block_count, BLK)
    slot_iota = jnp.arange(MAX_ACT).astype(jnp.int32)
    ranges = jnp.arange(N_DP).astype(jnp.int32)

    def one_block(packed):
        rows, ids, counts = packed
        flat = ids.reshape(-1)
        columns = jnp.take(up_blocks, flat, axis=1).reshape(D, -1)

        def add_range(total, index):
            start = index * width_part
            left = lax.dynamic_slice_in_dim(rows, start, width_part, 1)
            right = lax.dynamic_slice_in_dim(columns, start, width_part, 0)
            term = jnp.dot(left, right, preferred_element_type=jnp.float32)
            term = lax.optimization_barrier(term.astype(jnp.bfloat16)).astype(jnp.float32)
            return total + term, None

        start_total = jnp.zeros((BLK, N_TENSOR * MAX_ACT * BLK), jnp.float32)
        summed, _ = lax.scan(add_range, start_total, ranges)
        bias = jnp.take(bias_blocks, flat, axis=0).reshape(-1)
        live = (slot_iota[None, :] < counts[:, None]).astype(jnp.float32)
        live = jnp.repeat(live.reshape(-1), BLK)
        hidden = (jnp.maximum(summed + bias[None, :], 0.0) * live[None, :]).astype(jnp.bfloat16)
        weights_down = jnp.take(down_blocks, flat, axis=0).reshape(-1, D)
        return jnp.dot(hidden, weights_down, preferred_element_type=jnp.float32)

    outputs = lax.map(one_block, (rows_in.reshape(ROWS // BLK, BLK, D), active_ids, active_counts))
    return outputs.reshape(ROWS, D) + down_bias[None, :]
```

```python
import functools

import jax
import jax.numpy as jnp
from jax import lax
from jax.experimental import pallas as pl
from jax.experimental.pallas import tpu as pltpu
from jax.sharding import PartitionSpec as P

BLK = 128
ANY = pl.BlockSpec(memory_space=pl.ANY)
SMEM = pl.BlockSpec(memory_space=pltpu.SMEM)
VMEM = pl.BlockSpec(memory_space=pltpu.VMEM)
VMEM_LIMIT = 40 * 1024 * 1024


def place(flip, step, per_owner):
    if flip is None:
        return step
    return (lax.axis_index("tensor") ^ flip) * per_owner + step


def up_kernel(which, row0, ids, counts, rows, weight, out, x_buf, w_buf, sems):
    slots = ids.shape[2]
    per_shard = weight.shape[1] // BLK
    b = place(*which)
    count = counts[b, 0]

    def slab(s):
        block = lax.rem(ids[b, 0, s], per_shard)
        return pltpu.make_async_copy(
            weight.at[:, pl.ds(pl.multiple_of(block * BLK, BLK), BLK)],
            w_buf.at[:, pl.ds(s * BLK, BLK)],
            sems.at[s],
        )

    fetch = pltpu.make_async_copy(rows.at[pl.ds(row0, BLK)], x_buf, sems.at[slots])
    fetch.start()
    for s in range(slots):
        pl.when(s < count)(lambda s=s: slab(s).start())
    fetch.wait()
    for s in range(0, slots, 2):
        span = pl.ds(s * BLK, 2 * BLK)

        @pl.when(s < count)
        def _(s=s, span=span):
            slab(s).wait()
            pl.when(s + 1 < count)(lambda: slab(s + 1).wait())
            value = jnp.dot(x_buf[...], w_buf[:, span], preferred_element_type=jnp.float32)
            column = lax.broadcasted_iota(jnp.int32, value.shape, 1)
            live = (column < BLK) | (s + 1 < count)
            out[:, span] = jnp.where(live, value, 0.0).astype(out.dtype)

        @pl.when(s >= count)
        def _(span=span):
            out[:, span] = jnp.zeros((BLK, 2 * BLK), out.dtype)


def up(which, row0, ids, counts, rows, weight):
    slots = ids.shape[2]
    width = weight.shape[0]
    return pl.pallas_call(
        functools.partial(up_kernel, which, row0),
        out_shape=jax.ShapeDtypeStruct((BLK, slots * BLK), jnp.bfloat16),
        in_specs=[SMEM, SMEM, ANY, ANY],
        out_specs=VMEM,
        scratch_shapes=[
            pltpu.VMEM((BLK, width), jnp.bfloat16),
            pltpu.VMEM((width, slots * BLK), jnp.bfloat16),
            pltpu.SemaphoreType.DMA((slots + 1,)),
        ],
        compiler_params=pltpu.CompilerParams(vmem_limit_bytes=VMEM_LIMIT),
        cost_estimate=pl.CostEstimate(
            flops=2 * BLK * width * slots * BLK, bytes_accessed=2 * width * slots * BLK, transcendentals=0
        ),
        name="up",
    )(ids, counts, rows, weight)


def act_kernel(which, ids, counts, own, other, bias, out):
    slots = ids.shape[2]
    b = place(*which)
    count = counts[b, 0]
    per_shard = bias.shape[0]
    for s in range(slots):
        span = pl.ds(s * BLK, BLK)
        block = lax.rem(ids[b, 0, s], per_shard)
        value = own[:, span].astype(jnp.float32)
        if other is not None:
            value = value + other[:, span].astype(jnp.float32)
        value = jnp.maximum(value + bias[pl.ds(block, 1), :], 0.0)
        out[:, span] = jnp.where(s < count, value, 0.0).astype(out.dtype)


def activate(which, ids, counts, own, other, bias):
    body = act_kernel
    if other is None:
        body = lambda which, ids, counts, own, bias, out: act_kernel(which, ids, counts, own, None, bias, out)
    operands = [own] if other is None else [own, other]
    return pl.pallas_call(
        functools.partial(body, which),
        out_shape=jax.ShapeDtypeStruct(own.shape, jnp.bfloat16),
        in_specs=[SMEM, SMEM] + [VMEM] * len(operands) + [VMEM],
        out_specs=VMEM,
        cost_estimate=pl.CostEstimate(flops=own.size, bytes_accessed=6 * own.size, transcendentals=0),
        name="act",
    )(ids, counts, *operands, bias)


def down_kernel(which, row0, n_init, has_bias, has_base, two, ids, counts, *refs):
    refs = list(refs)
    hidden = refs.pop(0)
    other = refs.pop(0) if two else None
    weight = refs.pop(0)
    inits = [refs.pop(0) for _ in range(n_init)]
    bias = refs.pop(0) if has_bias else None
    if has_base:
        refs.pop(0)
    out, h_buf, w_buf, acc, out_buf, sems = refs
    slots = ids.shape[2]
    per_shard = weight.shape[0] // BLK
    b = place(*which)
    count = counts[b, 0]

    def slab(s):
        block = lax.rem(ids[b, 0, s], per_shard)
        return pltpu.make_async_copy(
            weight.at[pl.ds(pl.multiple_of(block * BLK, BLK), BLK)],
            w_buf.at[pl.ds(s * BLK, BLK)],
            sems.at[s],
        )

    def fetch(source):
        return pltpu.make_async_copy(source, h_buf, sems.at[slots])

    if two:
        z = lax.axis_index("dp")
        edge = (z != lax.axis_size("dp") // 2) & (z != lax.axis_size("dp") // 2 - 1)
        pl.when(edge)(lambda: fetch(other).start())
        pl.when(jnp.logical_not(edge))(lambda: fetch(hidden).start())
    else:
        fetch(hidden).start()
    for s in range(slots):
        pl.when(s < count)(lambda s=s: slab(s).start())
    start = jnp.zeros(acc.shape, jnp.float32)
    for init in inits:
        start = start + init[...].astype(jnp.float32)
    if bias is not None:
        start = start + bias[...]
    acc[...] = start
    fetch(hidden).wait()
    for s in range(0, slots, 2):

        @pl.when(s < count)
        def _(s=s):
            slab(s).wait()
            pl.when(s + 1 < count)(lambda: slab(s + 1).wait())

            @pl.when(s + 1 >= count)
            def _():
                w_buf[pl.ds((s + 1) * BLK, BLK), :] = jnp.zeros((BLK, w_buf.shape[1]), w_buf.dtype)

            acc[...] += jnp.dot(
                h_buf[:, pl.ds(s * BLK, 2 * BLK)],
                w_buf[pl.ds(s * BLK, 2 * BLK), :],
                preferred_element_type=jnp.float32,
            )

    out_buf[...] = acc[...].astype(out_buf.dtype)
    put = pltpu.make_async_copy(out_buf, out.at[pl.ds(row0, BLK)], sems.at[slots])
    put.start()
    put.wait()


def down(which, ids, counts, hidden, other, weight, inits=(), bias=None, base=None, rows=BLK, row0=0, dtype=jnp.bfloat16):
    slots = ids.shape[2]
    width = weight.shape[1]
    two = other is not None
    operands = [hidden] + ([other] if two else []) + [weight]
    specs = [ANY] * len(operands)
    operands += list(inits)
    specs += [VMEM] * len(inits)
    if bias is not None:
        operands.append(bias)
        specs.append(VMEM)
    aliases = {}
    if base is not None:
        operands.append(base)
        specs.append(ANY)
        aliases = {2 + len(operands) - 1: 0}
    return pl.pallas_call(
        functools.partial(down_kernel, which, row0, len(inits), bias is not None, base is not None, two),
        out_shape=jax.ShapeDtypeStruct((rows, width), dtype),
        in_specs=[SMEM, SMEM] + specs,
        out_specs=ANY,
        scratch_shapes=[
            pltpu.VMEM((BLK, slots * BLK), jnp.bfloat16),
            pltpu.VMEM((slots * BLK, width), jnp.bfloat16),
            pltpu.VMEM((BLK, width), jnp.float32),
            pltpu.VMEM((BLK, width), dtype),
            pltpu.SemaphoreType.DMA((slots + 1,)),
        ],
        input_output_aliases=aliases,
        compiler_params=pltpu.CompilerParams(vmem_limit_bytes=VMEM_LIMIT),
        cost_estimate=pl.CostEstimate(
            flops=2 * BLK * width * slots * BLK, bytes_accessed=2 * width * slots * BLK, transcendentals=0
        ),
        name="down",
    )(ids, counts, *operands)


def plain(rows_in, up_weight, up_bias, down_weight, down_bias, active_ids, active_counts):
    gathered = lax.all_gather(rows_in, "tensor", axis=0, tiled=True)
    blocks = gathered.shape[0] // BLK
    terms = []
    for b in range(blocks):
        which = (None, b, 1)
        part = up(which, b * BLK, active_ids, active_counts, gathered, up_weight)
        summed = lax.psum(part, "dp")
        hidden = activate(which, active_ids, active_counts, summed, None, up_bias.reshape(-1, BLK))
        terms.append(down(which, active_ids, active_counts, hidden, None, down_weight))
    terms = jnp.concatenate(terms, axis=0)
    owned = lax.psum_scatter(terms, "tensor", scatter_dimension=0, tiled=True).astype(jnp.float32)
    return owned + down_bias[None, :]


def staged(rows_in, up_weight, up_bias, down_weight, down_bias, active_ids, active_counts):
    per_owner = rows_in.shape[0] // BLK
    depth = lax.axis_size("dp")
    half = depth // 2
    bias_blocks = up_bias.reshape(-1, BLK)

    def swap(value, flip):
        return lax.ppermute(value, "tensor", [(t, t ^ flip) for t in range(4)])

    def hidden_of(which, row0, rows):
        value = up(which, row0, active_ids, active_counts, rows, up_weight)
        for hop in range(half - 1):
            moved = lax.ppermute(value, "dp", [(hop, hop + 1), (depth - 1 - hop, depth - 2 - hop)])
            value = (value.astype(jnp.float32) + moved.astype(jnp.float32)).astype(jnp.bfloat16)
        moved = lax.ppermute(value, "dp", [(half - 1, half), (half, half - 1)])
        hidden = activate(which, active_ids, active_counts, value, moved, bias_blocks)
        back = hidden
        for hop in range(half - 1, 0, -1):
            back = lax.ppermute(back, "dp", [(hop, hop - 1), (depth - 1 - hop, depth - hop)])
        return hidden, back

    def terms_of(which, pair, **more):
        return down(which, active_ids, active_counts, *pair, down_weight, **more)

    beside = swap(rows_in, 1)
    across = [swap(rows_in[j * BLK : (j + 1) * BLK], 3) for j in range(per_owner)]
    relayed = [swap(a, 1) for a in across]

    own = {}
    sums = {}
    near = {}
    far = {}
    base = None
    for j in range(per_owner):
        own[j] = hidden_of((0, j, per_owner), j * BLK, rows_in)
    for j in range(per_owner):
        pair3 = hidden_of((3, j, per_owner), 0, across[j])
        pair2 = hidden_of((2, j, per_owner), 0, relayed[j])
        sent = swap(terms_of((3, j, per_owner), pair3), 1)
        far[j] = swap(terms_of((2, j, per_owner), pair2, inits=[sent]), 2)
    for j in range(per_owner):
        pair1 = hidden_of((1, j, per_owner), j * BLK, beside)
        near[j] = swap(terms_of((1, j, per_owner), pair1), 1)
    for j in range(per_owner):
        base = terms_of(
            (0, j, per_owner),
            own[j],
            inits=[near[j], far[j]],
            bias=down_bias[None, :],
            base=base,
            rows=per_owner * BLK,
            row0=j * BLK,
            dtype=jnp.float32,
        )
    return base


def solution(mesh):
    placed = (
        P(("parts", "tensor"), "dp"),
        P("dp", "tensor"),
        P("tensor"),
        P("tensor", "dp"),
        P("dp"),
        P("parts", "tensor", None),
        P("parts", "tensor"),
    )

    def run(rows_in, *rest):
        whole_blocks = rows_in.shape[0] % BLK == 0
        if mesh.shape["tensor"] == 4 and mesh.shape["dp"] % 2 == 0 and whole_blocks:
            return staged(rows_in, *rest)
        return plain(rows_in, *rest)

    return jax.shard_map(
        run, mesh=mesh, in_specs=placed, out_specs=P(("parts", "tensor"), "dp"), check_vma=False
    )
```

```python
import functools

import jax
import jax.numpy as jnp
from jax import lax
from jax.experimental import pallas as pl
from jax.experimental.pallas import tpu as pltpu
from jax.sharding import PartitionSpec as P

BLK = 128
ANY = pl.BlockSpec(memory_space=pl.ANY)
SMEM = pl.BlockSpec(memory_space=pltpu.SMEM)
VMEM = pl.BlockSpec(memory_space=pltpu.VMEM)
MIB = 1024 * 1024
VMEM_LIMIT = 36 * MIB


def place(flip, step, per_owner):
    if flip is None:
        return step
    return (lax.axis_index("tensor") ^ flip) * per_owner + step


def up_kernel(which, row0, ids, counts, rows, weight, out, x_buf, w_buf, sems):
    slots = ids.shape[2]
    per_shard = weight.shape[1] // BLK
    b = place(*which)
    count = counts[b, 0]

    def slab(s):
        block = lax.rem(ids[b, 0, s], per_shard)
        return pltpu.make_async_copy(
            weight.at[:, pl.ds(pl.multiple_of(block * BLK, BLK), BLK)],
            w_buf.at[:, pl.ds(s * BLK, BLK)],
            sems.at[s],
        )

    fetch = pltpu.make_async_copy(rows.at[pl.ds(row0, BLK)], x_buf, sems.at[slots])
    fetch.start()
    for s in range(slots):
        pl.when(s < count)(lambda s=s: slab(s).start())
    fetch.wait()
    for s in range(0, slots, 2):
        span = pl.ds(s * BLK, 2 * BLK)

        @pl.when(s < count)
        def _(s=s, span=span):
            slab(s).wait()
            pl.when(s + 1 < count)(lambda: slab(s + 1).wait())
            value = jnp.dot(x_buf[...], w_buf[:, span], preferred_element_type=jnp.float32)
            column = lax.broadcasted_iota(jnp.int32, value.shape, 1)
            live = (column < BLK) | (s + 1 < count)
            out[:, span] = jnp.where(live, value, 0.0).astype(out.dtype)

        @pl.when(s >= count)
        def _(span=span):
            out[:, span] = jnp.zeros((BLK, 2 * BLK), out.dtype)


def up(which, row0, ids, counts, rows, weight):
    slots = ids.shape[2]
    width = weight.shape[0]
    return pl.pallas_call(
        functools.partial(up_kernel, which, row0),
        out_shape=jax.ShapeDtypeStruct((BLK, slots * BLK), jnp.bfloat16),
        in_specs=[SMEM, SMEM, ANY, ANY],
        out_specs=VMEM,
        scratch_shapes=[
            pltpu.VMEM((BLK, width), jnp.bfloat16),
            pltpu.VMEM((width, slots * BLK), jnp.bfloat16),
            pltpu.SemaphoreType.DMA((slots + 1,)),
        ],
        compiler_params=pltpu.CompilerParams(vmem_limit_bytes=VMEM_LIMIT),
        cost_estimate=pl.CostEstimate(
            flops=2 * BLK * width * slots * BLK, bytes_accessed=2 * width * slots * BLK, transcendentals=0
        ),
        name="up",
    )(ids, counts, rows, weight)


def bias_kernel(order, ids, counts, bias, out):
    slots = ids.shape[2]
    per_shard = bias.shape[0]
    for c, which in enumerate(order):
        b = place(*which)
        for s in range(slots):
            row = bias[pl.ds(lax.rem(ids[b, 0, s], per_shard), 1), :]
            out[pl.ds(c, 1), pl.ds(s * BLK, BLK)] = jnp.where(s < counts[b, 0], row, 0.0)


def bias_table(order, ids, counts, bias):
    slots = ids.shape[2]
    return pl.pallas_call(
        functools.partial(bias_kernel, order),
        out_shape=jax.ShapeDtypeStruct((len(order), slots * BLK), jnp.float32),
        in_specs=[SMEM, SMEM, VMEM],
        out_specs=VMEM,
        compiler_params=pltpu.CompilerParams(vmem_limit_bytes=MIB),
        cost_estimate=pl.CostEstimate(flops=bias.size, bytes_accessed=8 * bias.size, transcendentals=0),
        name="bias_table",
    )(ids, counts, bias)


def down_kernel(which, row0, n_init, has_bias, has_base, two, ids, counts, *refs):
    refs = list(refs)
    hidden = refs.pop(0)
    other = refs.pop(0) if two else None
    weight = refs.pop(0)
    inits = [refs.pop(0) for _ in range(n_init)]
    bias = refs.pop(0) if has_bias else None
    if has_base:
        refs.pop(0)
    out, h_buf, w_buf, acc, out_buf, sems = refs
    slots = ids.shape[2]
    per_shard = weight.shape[0] // BLK
    b = place(*which)
    count = counts[b, 0]

    def slab(s):
        block = lax.rem(ids[b, 0, s], per_shard)
        return pltpu.make_async_copy(
            weight.at[pl.ds(pl.multiple_of(block * BLK, BLK), BLK)],
            w_buf.at[pl.ds(s * BLK, BLK)],
            sems.at[s],
        )

    def fetch(source):
        return pltpu.make_async_copy(source, h_buf, sems.at[slots])

    if two:
        z = lax.axis_index("dp")
        edge = (z != lax.axis_size("dp") // 2) & (z != lax.axis_size("dp") // 2 - 1)
        pl.when(edge)(lambda: fetch(other).start())
        pl.when(jnp.logical_not(edge))(lambda: fetch(hidden).start())
    else:
        fetch(hidden).start()
    for s in range(slots):
        pl.when(s < count)(lambda s=s: slab(s).start())
    start = jnp.zeros(acc.shape, jnp.float32)
    for init in inits:
        start = start + init[...].astype(jnp.float32)
    if bias is not None:
        start = start + bias[...]
    acc[...] = start
    fetch(hidden).wait()
    for s in range(0, slots, 2):

        @pl.when(s < count)
        def _(s=s):
            slab(s).wait()
            pl.when(s + 1 < count)(lambda: slab(s + 1).wait())

            @pl.when(s + 1 >= count)
            def _():
                w_buf[pl.ds((s + 1) * BLK, BLK), :] = jnp.zeros((BLK, w_buf.shape[1]), w_buf.dtype)

            acc[...] += jnp.dot(
                h_buf[:, pl.ds(s * BLK, 2 * BLK)],
                w_buf[pl.ds(s * BLK, 2 * BLK), :],
                preferred_element_type=jnp.float32,
            )

    out_buf[...] = acc[...].astype(out_buf.dtype)
    put = pltpu.make_async_copy(out_buf, out.at[pl.ds(row0, BLK)], sems.at[slots])
    put.start()
    put.wait()


def down(which, ids, counts, hidden, other, weight, inits=(), bias=None, base=None, rows=BLK, row0=0, dtype=jnp.bfloat16):
    slots = ids.shape[2]
    width = weight.shape[1]
    two = other is not None
    operands = [hidden] + ([other] if two else []) + [weight]
    specs = [ANY] * len(operands)
    operands += list(inits)
    specs += [VMEM] * len(inits)
    if bias is not None:
        operands.append(bias)
        specs.append(VMEM)
    aliases = {}
    if base is not None:
        operands.append(base)
        specs.append(ANY)
        aliases = {2 + len(operands) - 1: 0}
    return pl.pallas_call(
        functools.partial(down_kernel, which, row0, len(inits), bias is not None, base is not None, two),
        out_shape=jax.ShapeDtypeStruct((rows, width), dtype),
        in_specs=[SMEM, SMEM] + specs,
        out_specs=ANY,
        scratch_shapes=[
            pltpu.VMEM((BLK, slots * BLK), jnp.bfloat16),
            pltpu.VMEM((slots * BLK, width), jnp.bfloat16),
            pltpu.VMEM((BLK, width), jnp.float32),
            pltpu.VMEM((BLK, width), dtype),
            pltpu.SemaphoreType.DMA((slots + 1,)),
        ],
        input_output_aliases=aliases,
        compiler_params=pltpu.CompilerParams(vmem_limit_bytes=VMEM_LIMIT),
        cost_estimate=pl.CostEstimate(
            flops=2 * BLK * width * slots * BLK, bytes_accessed=2 * width * slots * BLK, transcendentals=0
        ),
        name="down",
    )(ids, counts, *operands)


def active(total, bias):
    return jnp.maximum(total + bias, 0.0).astype(jnp.bfloat16)


def plain(rows_in, up_weight, up_bias, down_weight, down_bias, active_ids, active_counts):
    gathered = lax.all_gather(rows_in, "tensor", axis=0, tiled=True)
    order = [(None, b, 1) for b in range(gathered.shape[0] // BLK)]
    table = bias_table(order, active_ids, active_counts, up_bias.reshape(-1, BLK))
    terms = []
    for b, which in enumerate(order):
        part = up(which, b * BLK, active_ids, active_counts, gathered, up_weight)
        summed = lax.psum(part, "dp").astype(jnp.float32)
        hidden = active(summed, table[b : b + 1])
        terms.append(down(which, active_ids, active_counts, hidden, None, down_weight))
    terms = jnp.concatenate(terms, axis=0)
    owned = lax.psum_scatter(terms, "tensor", scatter_dimension=0, tiled=True).astype(jnp.float32)
    return owned + down_bias[None, :]


def staged(rows_in, up_weight, up_bias, down_weight, down_bias, active_ids, active_counts):
    f32 = jnp.float32
    order = [(0, 0, 2), (1, 0, 2), (3, 0, 2), (2, 0, 2), (3, 1, 2), (2, 1, 2), (1, 1, 2), (0, 1, 2)]
    steps = len(order)
    lag = 3
    position = lax.axis_index("dp")
    edge = (position == 0) | (position == 3)

    def swap(value, flip):
        return lax.ppermute(value, "tensor", [(t, t ^ flip) for t in range(4)])

    across = [swap(rows_in[:BLK], 3), swap(rows_in[BLK:], 3)]
    beside = swap(rows_in, 1)
    relayed = [swap(a, 1) for a in across]
    table = bias_table(order, active_ids, active_counts, up_bias.reshape(-1, BLK))
    source = {0: (rows_in, BLK), 1: (beside, BLK), 2: (relayed, 0), 3: (across, 0)}

    def up_step(i):
        flip, j, _ = order[i]
        rows, stride = source[flip]
        rows = rows[j] if stride == 0 else rows
        return up(order[i], j * stride, active_ids, active_counts, rows, up_weight)

    def down_step(i, pair, **more):
        return down(order[i], active_ids, active_counts, *pair, down_weight, **more)

    hidden, terms, near, far = {}, {}, {}, {}
    base = None
    for i in range(steps + lag):
        back = i - lag
        part = up_step(i) if i < steps else None
        if part is None:
            sent = hidden[back]
        elif back < 0:
            sent = part
        else:
            sent = jnp.where(edge, part, hidden[back])
        got = lax.ppermute(sent, "dp", [(0, 1), (1, 0), (2, 3), (3, 2)])
        if part is not None:
            folded = (part.astype(f32) + got.astype(f32)).astype(jnp.bfloat16)
            other = lax.ppermute(folded, "dp", [(1, 2), (2, 1)])
            hidden[i] = active(folded.astype(f32) + other.astype(f32), table[i : i + 1])
        if back >= 0:
            flip, j, _ = order[back]
            pair = (hidden[back], got)
            if flip == 1:
                near[j] = swap(down_step(back, pair), 1)
            elif flip == 3:
                terms[j] = swap(down_step(back, pair), 1)
            elif flip == 2:
                far[j] = swap(down_step(back, pair, inits=[terms[j]]), 2)
            else:
                terms[j, "own"] = (back, pair)
            if j == 1 and flip == 0:
                for row in range(2):
                    base = down_step(
                        *terms[row, "own"],
                        inits=[near[row], far[row]],
                        bias=down_bias[None, :],
                        base=base,
                        rows=2 * BLK,
                        row0=row * BLK,
                        dtype=f32,
                    )
    return base


def solution(mesh):
    placed = (
        P(("parts", "tensor"), "dp"),
        P("dp", "tensor"),
        P("tensor"),
        P("tensor", "dp"),
        P("dp"),
        P("parts", "tensor", None),
        P("parts", "tensor"),
    )

    def run(rows_in, *rest):
        if mesh.shape["tensor"] == 4 and mesh.shape["dp"] == 4 and rows_in.shape[0] == 2 * BLK:
            return staged(rows_in, *rest)
        return plain(rows_in, *rest)

    return jax.shard_map(
        run, mesh=mesh, in_specs=placed, out_specs=P(("parts", "tensor"), "dp"), check_vma=False
    )
```

```python
import functools

import jax
import jax.numpy as jnp
from jax import lax
from jax.experimental import pallas as pl
from jax.experimental.pallas import tpu as pltpu
from jax.sharding import PartitionSpec as P

BLK = 128
ANY = pl.BlockSpec(memory_space=pl.ANY)
SMEM = pl.BlockSpec(memory_space=pltpu.SMEM)
VMEM = pl.BlockSpec(memory_space=pltpu.VMEM)
MIB = 1024 * 1024
COST = 1
VMEM_LIMIT = 36 * MIB


def place(flip, step, per_owner):
    if flip is None:
        return step
    return (lax.axis_index("tensor") ^ flip) * per_owner + step


def projection(b, ids, counts, weight, x_buf, out, w_buf, sem):
    slots = ids.shape[2]
    per_shard = weight.shape[1] // BLK
    count = counts[0, b]

    def slab(s):
        block = lax.rem(ids[b, 0, s], per_shard)
        return pltpu.make_async_copy(
            weight.at[:, pl.ds(pl.multiple_of(block * BLK, BLK), BLK)],
            w_buf.at[:, pl.ds(s * BLK, BLK)],
            sem(s),
        )

    def start():
        for s in range(slots):
            pl.when(s < count)(lambda s=s: slab(s).start())

    def finish():
        for s in range(0, slots, 2):
            span = pl.ds(s * BLK, 2 * BLK)

            @pl.when(s < count)
            def _(s=s, span=span):
                slab(s).wait()
                pl.when(s + 1 < count)(lambda: slab(s + 1).wait())
                value = jnp.dot(x_buf[...], w_buf[:, span], preferred_element_type=jnp.float32)
                column = lax.broadcasted_iota(jnp.int32, value.shape, 1)
                live = (column < BLK) | (s + 1 < count)
                out[:, span] = jnp.where(live, value, 0.0).astype(out.dtype)

            @pl.when(s >= count)
            def _(span=span):
                out[:, span] = jnp.zeros((BLK, 2 * BLK), out.dtype)

    return start, finish


def fill_table(order, ids, counts, bias, out):
    slots = ids.shape[2]
    per_shard = bias.shape[0]
    for c, which in enumerate(order):
        b = place(*which)
        for s in range(slots):
            row = bias[pl.ds(lax.rem(ids[b, 0, s], per_shard), 1), :]
            out[pl.ds(c, 1), pl.ds(s * BLK, BLK)] = jnp.where(s < counts[0, b], row, 0.0)


def head_kernel(order, ids, counts, rows, weight, bias, out, low, high, table, w_buf, sems):
    slots = ids.shape[2]
    halves = [
        pltpu.make_async_copy(rows.at[pl.ds(j * BLK, BLK)], half, sems.at[slots + j])
        for j, half in enumerate((low, high))
    ]

    start, finish = projection(
        place(*order[0]), ids, counts, weight, low, out, w_buf, lambda s: sems.at[s]
    )
    for half in halves:
        half.start()
    start()
    fill_table(order, ids, counts, bias, table)
    for half in halves:
        half.wait()
    finish()


def head(order, ids, counts, rows, weight, bias):
    slots = ids.shape[2]
    width = weight.shape[0]
    return pl.pallas_call(
        functools.partial(head_kernel, order),
        out_shape=[
            jax.ShapeDtypeStruct((BLK, slots * BLK), jnp.bfloat16),
            jax.ShapeDtypeStruct((BLK, width), jnp.bfloat16),
            jax.ShapeDtypeStruct((BLK, width), jnp.bfloat16),
            jax.ShapeDtypeStruct((len(order), slots * BLK), jnp.float32),
        ],
        in_specs=[SMEM, SMEM, ANY, ANY, VMEM],
        out_specs=[VMEM] * 4,
        scratch_shapes=[
            pltpu.VMEM((width, slots * BLK), jnp.bfloat16),
            pltpu.SemaphoreType.DMA((slots + 2,)),
        ],
        compiler_params=pltpu.CompilerParams(vmem_limit_bytes=62 * MIB),
        cost_estimate=pl.CostEstimate(flops=COST, bytes_accessed=COST, transcendentals=0),
        name="head",
    )(ids, counts, rows, weight, bias)


def up_kernel(blocks, n_after, n_keep, ids, counts, weight, *refs):
    n_rows = [n for _, n in blocks]
    rows, refs = refs[: sum(n_rows)], refs[sum(n_rows) + n_after :]
    outs, kept = refs[: len(blocks)], refs[len(blocks) : len(blocks) + n_keep]
    x_buf, w_buf, sems, row_sems = refs[len(blocks) + n_keep :]
    fetches, steps = [], []
    for k, (which, n) in enumerate(blocks):
        height = BLK // n
        for part in range(n):
            at = len(fetches)
            fetches.append(
                pltpu.make_async_copy(
                    rows[at], x_buf.at[k, pl.ds(part * height, height)], row_sems.at[at]
                )
            )
        steps.append(
            projection(
                place(*which),
                ids,
                counts,
                weight,
                x_buf.at[k],
                outs[k],
                w_buf.at[k],
                lambda s, k=k: sems.at[k, s],
            )
        )
    for fetch in fetches:
        fetch.start()
    for start, _ in steps:
        start()
    for fetch in fetches:
        fetch.wait()
    for k, part in enumerate(kept):
        part[...] = x_buf[0, pl.ds(k * part.shape[0], part.shape[0]), :]
    for _, finish in steps:
        finish()


def up(whiches, ids, counts, rows, weight, after=(), keep=0):
    slots = ids.shape[2]
    width = weight.shape[0]
    count = len(whiches)
    parts = [part for block in rows for part in block]
    return pl.pallas_call(
        functools.partial(up_kernel, [(w, len(r)) for w, r in zip(whiches, rows)], len(after), keep),
        out_shape=[jax.ShapeDtypeStruct((BLK, slots * BLK), jnp.bfloat16)] * count
        + [jax.ShapeDtypeStruct((BLK // max(keep, 1), width), jnp.bfloat16)] * keep,
        in_specs=[SMEM, SMEM] + [ANY] * (1 + len(parts) + len(after)),
        out_specs=[VMEM] * (count + keep),
        scratch_shapes=[
            pltpu.VMEM((count, BLK, width), jnp.bfloat16),
            pltpu.VMEM((count, width, slots * BLK), jnp.bfloat16),
            pltpu.SemaphoreType.DMA((count, slots)),
            pltpu.SemaphoreType.DMA((len(parts),)),
        ],
        compiler_params=pltpu.CompilerParams(vmem_limit_bytes=VMEM_LIMIT),
        cost_estimate=pl.CostEstimate(flops=COST, bytes_accessed=COST, transcendentals=0),
        name="up",
    )(ids, counts, weight, *parts, *after)


def bias_table(order, ids, counts, bias):
    slots = ids.shape[2]
    return pl.pallas_call(
        functools.partial(fill_table, order),
        out_shape=jax.ShapeDtypeStruct((len(order), slots * BLK), jnp.float32),
        in_specs=[SMEM, SMEM, VMEM],
        out_specs=VMEM,
        compiler_params=pltpu.CompilerParams(vmem_limit_bytes=MIB),
        cost_estimate=pl.CostEstimate(flops=COST, bytes_accessed=COST, transcendentals=0),
        name="bias_table",
    )(ids, counts, bias)


def down_kernel(whiches, n_init, has_bias, n_after, two, n_parts, ids, counts, *refs):
    refs = list(refs)

    def take(n):
        taken = refs[:n]
        del refs[:n]
        return taken

    pairs = [take(2 if two else 1) for _ in whiches]
    (weight,) = take(1)
    inits = take(n_init)
    bias = take(has_bias)
    take(n_after)
    outs = [take(n_parts) for _ in whiches]
    h_buf, w_buf, acc, sems = refs
    slots = ids.shape[2]
    per_shard = weight.shape[0] // BLK
    position = lax.axis_index("dp")
    edge = (position == 0) | (position == lax.axis_size("dp") - 1)

    def slab(k, s):
        block = lax.rem(ids[place(*whiches[k]), 0, s], per_shard)
        return pltpu.make_async_copy(
            weight.at[pl.ds(pl.multiple_of(block * BLK, BLK), BLK)],
            w_buf.at[k, pl.ds(s * BLK, BLK)],
            sems.at[k, s],
        )

    def fetch(k, source):
        return pltpu.make_async_copy(source, h_buf.at[k], sems.at[k, slots])

    for k, which in enumerate(whiches):
        if two:
            pl.when(edge)(lambda k=k: fetch(k, pairs[k][1]).start())
            pl.when(jnp.logical_not(edge))(lambda k=k: fetch(k, pairs[k][0]).start())
        else:
            fetch(k, pairs[k][0]).start()
        for s in range(slots):
            pl.when(s < counts[0, place(*which)])(lambda k=k, s=s: slab(k, s).start())
    for k in range(len(whiches)):
        if bias and whiches[k][0] == 0:
            acc[k] = jnp.broadcast_to(bias[0][...], acc.shape[1:])
        elif not inits:
            acc[k] = jnp.zeros(acc.shape[1:], jnp.float32)
    for at, init in enumerate(inits):
        acc[0, pl.ds(at * init.shape[0], init.shape[0]), :] = init[...].astype(jnp.float32)
    for k, which in enumerate(whiches):
        count = counts[0, place(*which)]
        fetch(k, pairs[k][0]).wait()
        for s in range(0, slots, 2):

            @pl.when(s < count)
            def _(k=k, s=s, count=count):
                slab(k, s).wait()
                pl.when(s + 1 < count)(lambda: slab(k, s + 1).wait())

                @pl.when(s + 1 >= count)
                def _():
                    w_buf[k, pl.ds((s + 1) * BLK, BLK), :] = jnp.zeros((BLK, w_buf.shape[2]), w_buf.dtype)

                acc[k] += jnp.dot(
                    h_buf[k, :, pl.ds(s * BLK, 2 * BLK)],
                    w_buf[k, pl.ds(s * BLK, 2 * BLK), :],
                    preferred_element_type=jnp.float32,
                )

        for at, out in enumerate(outs[k]):
            out[...] = acc[k, pl.ds(at * out.shape[0], out.shape[0]), :].astype(out.dtype)


def down(whiches, ids, counts, pairs, weight, inits=(), bias=None, after=(), dtypes=(jnp.bfloat16,), parts=1):
    slots = ids.shape[2]
    width = weight.shape[1]
    count = len(whiches)
    two = len(pairs[0]) == 2
    extra = list(inits) + ([] if bias is None else [bias])
    out = pl.pallas_call(
        functools.partial(down_kernel, whiches, len(inits), bias is not None, len(after), two, parts),
        out_shape=[jax.ShapeDtypeStruct((BLK // parts, width), dtype) for dtype in dtypes for _ in range(parts)],
        in_specs=[SMEM, SMEM] + [ANY] * (count * len(pairs[0]) + 1) + [VMEM] * len(extra) + [ANY] * len(after),
        out_specs=[VMEM] * (parts * count),
        scratch_shapes=[
            pltpu.VMEM((count, BLK, slots * BLK), jnp.bfloat16),
            pltpu.VMEM((count, slots * BLK, width), jnp.bfloat16),
            pltpu.VMEM((count, BLK, width), jnp.float32),
            pltpu.SemaphoreType.DMA((count, slots + 1)),
        ],
        compiler_params=pltpu.CompilerParams(vmem_limit_bytes=VMEM_LIMIT),
        cost_estimate=pl.CostEstimate(flops=COST, bytes_accessed=COST, transcendentals=0),
        name="down",
    )(ids, counts, *[x for pair in pairs for x in pair], weight, *extra, *after)
    return [out[k * parts : (k + 1) * parts] for k in range(count)]


def active(total, bias):
    return jnp.maximum(total + bias, 0.0).astype(jnp.bfloat16)


def small(body, name, outs, operands, after):
    def run(*refs):
        body(*refs[: len(operands)], *refs[len(operands) + len(after) :])

    return pl.pallas_call(
        run,
        out_shape=outs,
        in_specs=[VMEM] * len(operands) + [ANY] * len(after),
        out_specs=jax.tree.map(lambda _: VMEM, outs),
        compiler_params=pltpu.CompilerParams(vmem_limit_bytes=VMEM_LIMIT),
        cost_estimate=pl.CostEstimate(flops=COST, bytes_accessed=COST, transcendentals=0),
        name=name,
    )(*operands, *after)


def fold(part, got, after):
    def body(part, got, out):
        out[...] = (part[...].astype(jnp.float32) + got[...].astype(jnp.float32)).astype(out.dtype)

    return small(body, "fold", jax.ShapeDtypeStruct(part.shape, part.dtype), [part, got], after)


def mix(i, folded, other, table, part, after):
    shape = jax.ShapeDtypeStruct(folded.shape, folded.dtype)

    def body(folded, other, table, *refs):
        total = folded[...].astype(jnp.float32) + other[...].astype(jnp.float32)
        value = active(total, table[i : i + 1, :])
        refs[-1][...] = value
        if part is not None:
            position = lax.axis_index("dp")
            edge = (position == 0) | (position == lax.axis_size("dp") - 1)
            out = refs[1]

            @pl.when(edge)
            def _():
                out[...] = refs[0][...]

            @pl.when(jnp.logical_not(edge))
            def _():
                out[...] = value

    if part is None:
        value = small(body, "mix", shape, [folded, other, table], after)
        return value, value
    sent, value = small(body, "mix", [shape, shape], [folded, other, table, part], after)
    return value, sent


def plain(rows_in, up_weight, up_bias, down_weight, down_bias, active_ids, active_counts):
    gathered = lax.all_gather(rows_in, "tensor", axis=0, tiled=True)
    order = [(None, b, 1) for b in range(gathered.shape[0] // BLK)]
    table = bias_table(order, active_ids, active_counts, up_bias.reshape(-1, BLK))
    terms = []
    for b, which in enumerate(order):
        (part,) = up([which], active_ids, active_counts, [[gathered[b * BLK : (b + 1) * BLK]]], up_weight)
        summed = lax.psum(part, "dp").astype(jnp.float32)
        hidden = active(summed, table[b : b + 1])
        terms.append(down([which], active_ids, active_counts, [[hidden]], down_weight)[0][0])
    terms = jnp.concatenate(terms, axis=0)
    owned = lax.psum_scatter(terms, "tensor", scatter_dimension=0, tiled=True).astype(jnp.float32)
    return owned + down_bias[None, :]


def staged(rows_in, up_weight, up_bias, down_weight, down_bias, active_ids, active_counts):
    f32 = jnp.float32
    order = [(f, j, 2) for f, j in ((0, 0), (1, 0), (0, 1), (3, 0), (2, 0), (3, 1), (2, 1), (1, 1))]
    steps = len(order)
    lag = 3

    def swap(parts, flip):
        return [lax.ppermute(part, "tensor", [(t, t ^ flip) for t in range(4)]) for part in parts]

    first, low, high, table = head(
        order, active_ids, active_counts, rows_in, up_weight, up_bias.reshape(-1, BLK)
    )
    mine = [[low], [high]]
    across = [swap(block, 3) for block in mine]
    beside = [swap(block, 1) for block in mine]
    relayed = {}
    source = {0: mine, 1: beside, 2: relayed, 3: across}
    partial, folded, other, hidden, got, terms, near, far, own = {0: first}, {}, {}, {}, {}, {}, {}, {}, {}
    after = first
    line = []

    def do_up(some, after, keep=0):
        rows = [source[order[i][0]][order[i][1]] for i in some]
        out = up([order[i] for i in some], active_ids, active_counts, rows, up_weight, [after], keep)
        partial.update(zip(some, out))
        return out[len(some) :]

    def do_down(some, after, **more):
        pairs = [(hidden[i], got[i + lag]) for i in some]
        return down([order[i] for i in some], active_ids, active_counts, pairs, down_weight, after=after, **more)

    ups = {0: [(1, 2, 7)], 2: [(3,)], 3: [(4,)], 4: [(5,)], 5: [(6,)]}
    downs = {7: [(3,)], 8: [(4,)], 9: [(5,)], 10: [(6,)], 11: [(7,), (0, 1, 2)]}
    for i in range(steps + lag + 1):
        back = i - lag
        latest = after
        if i < steps + lag:
            sent = partial.get(i)
            if back >= 0:
                hidden[back], sent = mix(back, folded[back], other[back], table, partial.get(i), [])
                latest = sent
            got[i] = lax.ppermute(sent, "dp", [(0, 1), (1, 0), (2, 3), (3, 2)])
        for some in ups.get(i, ()):
            flip, j, _ = order[some[0]]
            rows = do_up(some, partial[some[0] - 1], 2 if flip == 3 else 0)
            latest = partial[some[0]]
            if flip == 3:
                relayed[j] = swap(rows, 1)
        if 0 <= i - 1 < steps:
            latest = folded[i - 1] = fold(partial[i - 1], got[i - 1], [])
            other[i - 1] = lax.ppermute(latest, "dp", [(1, 2), (2, 1)])
        for some in downs.get(i, ()):
            flip, j, _ = order[some[0]]
            if flip == 0:
                dtypes = [f32 if order[k][0] == 0 else jnp.bfloat16 for k in some]
                out = do_down(some, [latest] + line + far[0], bias=down_bias[None, :], dtypes=dtypes)
                for k, value in zip(some, out):
                    flip, j, _ = order[k]
                    if flip == 0:
                        own[j] = value[0]
                    else:
                        near[j] = swap(value, 1)
                latest = out[0][0]
                line = [latest]
                continue
            (out,) = do_down(some, [latest] + line, inits=terms[j] if flip == 2 else (), parts=2)
            latest = out[0]
            line = [latest]
            {1: near, 2: far, 3: terms}[flip][j] = swap(out, 2 if flip == 2 else 1)
        after = latest

    def joined(parts):
        return jnp.concatenate(parts, axis=0).astype(f32)

    return jnp.concatenate([own[j] + joined(near[j]) + joined(far[j]) for j in range(2)], axis=0)


def solution(mesh):
    placed = (
        P(("parts", "tensor"), "dp"),
        P("dp", "tensor"),
        P("tensor"),
        P("tensor", "dp"),
        P("dp"),
        P("parts", "tensor", None),
        P("parts", "tensor"),
    )

    def run(rows_in, up_weight, up_bias, down_weight, down_bias, active_ids, active_counts):
        rest = (up_weight, up_bias, down_weight, down_bias, active_ids, active_counts.T)
        if mesh.shape["tensor"] == 4 and mesh.shape["dp"] == 4 and rows_in.shape[0] == 2 * BLK:
            return staged(rows_in, *rest)
        return plain(rows_in, *rest)

    return jax.shard_map(
        run, mesh=mesh, in_specs=placed, out_specs=P(("parts", "tensor"), "dp"), check_vma=False
    )
```

```python
import functools

import jax
import jax.numpy as jnp
from jax import lax
from jax.experimental import pallas as pl
from jax.experimental.pallas import tpu as pltpu
from jax.sharding import PartitionSpec as P

BLK = 128
ANY = pl.BlockSpec(memory_space=pl.ANY)
SMEM = pl.BlockSpec(memory_space=pltpu.SMEM)
VMEM = pl.BlockSpec(memory_space=pltpu.VMEM)
MIB = 1024 * 1024
COST = 1
VMEM_LIMIT = 36 * MIB


def place(flip, step, per_owner):
    if flip is None:
        return step
    return (lax.axis_index("tensor") ^ flip) * per_owner + step


def projection(b, ids, counts, weight, x_buf, out, w_buf, sem):
    slots = ids.shape[2]
    per_shard = weight.shape[1] // BLK
    count = counts[0, b]

    def slab(s):
        block = lax.rem(ids[b, 0, s], per_shard)
        return pltpu.make_async_copy(
            weight.at[:, pl.ds(pl.multiple_of(block * BLK, BLK), BLK)],
            w_buf.at[:, pl.ds(s * BLK, BLK)],
            sem(s),
        )

    def start():
        for s in range(slots):
            pl.when(s < count)(lambda s=s: slab(s).start())

    def finish():
        for s in range(0, slots, 2):
            span = pl.ds(s * BLK, 2 * BLK)

            @pl.when(s < count)
            def _(s=s, span=span):
                slab(s).wait()
                pl.when(s + 1 < count)(lambda: slab(s + 1).wait())
                value = jnp.dot(x_buf[...], w_buf[:, span], preferred_element_type=jnp.float32)
                column = lax.broadcasted_iota(jnp.int32, value.shape, 1)
                live = (column < BLK) | (s + 1 < count)
                out[:, span] = jnp.where(live, value, 0.0).astype(out.dtype)

            @pl.when(s >= count)
            def _(span=span):
                out[:, span] = jnp.zeros((BLK, 2 * BLK), out.dtype)

    return start, finish


def fill_table(order, ids, counts, bias, out):
    slots = ids.shape[2]
    per_shard = bias.shape[0]
    for c, which in enumerate(order):
        b = place(*which)
        for s in range(slots):
            row = bias[pl.ds(lax.rem(ids[b, 0, s], per_shard), 1), :]
            out[pl.ds(c, 1), pl.ds(s * BLK, BLK)] = jnp.where(s < counts[0, b], row, 0.0)


def head_kernel(order, ids, counts, rows, weight, bias, out, low, high, table, w_buf, sems):
    slots = ids.shape[2]
    halves = [
        pltpu.make_async_copy(rows.at[pl.ds(j * BLK, BLK)], half, sems.at[slots + j])
        for j, half in enumerate((low, high))
    ]

    start, finish = projection(
        place(*order[0]), ids, counts, weight, low, out, w_buf, lambda s: sems.at[s]
    )
    for half in halves:
        half.start()
    start()
    fill_table(order, ids, counts, bias, table)
    for half in halves:
        half.wait()
    finish()


def head(order, ids, counts, rows, weight, bias):
    slots = ids.shape[2]
    width = weight.shape[0]
    return pl.pallas_call(
        functools.partial(head_kernel, order),
        out_shape=[
            jax.ShapeDtypeStruct((BLK, slots * BLK), jnp.bfloat16),
            jax.ShapeDtypeStruct((BLK, width), jnp.bfloat16),
            jax.ShapeDtypeStruct((BLK, width), jnp.bfloat16),
            jax.ShapeDtypeStruct((len(order), slots * BLK), jnp.float32),
        ],
        in_specs=[SMEM, SMEM, ANY, ANY, VMEM],
        out_specs=[VMEM] * 4,
        scratch_shapes=[
            pltpu.VMEM((width, slots * BLK), jnp.bfloat16),
            pltpu.SemaphoreType.DMA((slots + 2,)),
        ],
        compiler_params=pltpu.CompilerParams(vmem_limit_bytes=62 * MIB),
        cost_estimate=pl.CostEstimate(flops=COST, bytes_accessed=COST, transcendentals=0),
        name="head",
    )(ids, counts, rows, weight, bias)


def up_kernel(blocks, n_after, n_keep, ids, counts, weight, *refs):
    n_rows = [n for _, n in blocks]
    rows, refs = refs[: sum(n_rows)], refs[sum(n_rows) + n_after :]
    outs, kept = refs[: len(blocks)], refs[len(blocks) : len(blocks) + n_keep]
    x_buf, w_buf, sems, row_sems = refs[len(blocks) + n_keep :]
    fetches, steps = [], []
    for k, (which, n) in enumerate(blocks):
        height = BLK // n
        for part in range(n):
            at = len(fetches)
            fetches.append(
                pltpu.make_async_copy(
                    rows[at], x_buf.at[k, pl.ds(part * height, height)], row_sems.at[at]
                )
            )
        steps.append(
            projection(
                place(*which),
                ids,
                counts,
                weight,
                x_buf.at[k],
                outs[k],
                w_buf.at[k],
                lambda s, k=k: sems.at[k, s],
            )
        )
    for fetch in fetches:
        fetch.start()
    for start, _ in steps:
        start()
    for fetch in fetches:
        fetch.wait()
    for k, part in enumerate(kept):
        part[...] = x_buf[0, pl.ds(k * part.shape[0], part.shape[0]), :]
    for _, finish in steps:
        finish()


def up(whiches, ids, counts, rows, weight, after=(), keep=0):
    slots = ids.shape[2]
    width = weight.shape[0]
    count = len(whiches)
    parts = [part for block in rows for part in block]
    return pl.pallas_call(
        functools.partial(up_kernel, [(w, len(r)) for w, r in zip(whiches, rows)], len(after), keep),
        out_shape=[jax.ShapeDtypeStruct((BLK, slots * BLK), jnp.bfloat16)] * count
        + [jax.ShapeDtypeStruct((BLK // max(keep, 1), width), jnp.bfloat16)] * keep,
        in_specs=[SMEM, SMEM] + [ANY] * (1 + len(parts) + len(after)),
        out_specs=[VMEM] * (count + keep),
        scratch_shapes=[
            pltpu.VMEM((count, BLK, width), jnp.bfloat16),
            pltpu.VMEM((count, width, slots * BLK), jnp.bfloat16),
            pltpu.SemaphoreType.DMA((count, slots)),
            pltpu.SemaphoreType.DMA((len(parts),)),
        ],
        compiler_params=pltpu.CompilerParams(vmem_limit_bytes=VMEM_LIMIT),
        cost_estimate=pl.CostEstimate(flops=COST, bytes_accessed=COST, transcendentals=0),
        name="up",
    )(ids, counts, weight, *parts, *after)


def bias_table(order, ids, counts, bias):
    slots = ids.shape[2]
    return pl.pallas_call(
        functools.partial(fill_table, order),
        out_shape=jax.ShapeDtypeStruct((len(order), slots * BLK), jnp.float32),
        in_specs=[SMEM, SMEM, VMEM],
        out_specs=VMEM,
        compiler_params=pltpu.CompilerParams(vmem_limit_bytes=MIB),
        cost_estimate=pl.CostEstimate(flops=COST, bytes_accessed=COST, transcendentals=0),
        name="bias_table",
    )(ids, counts, bias)


def down_kernel(whiches, n_init, has_bias, n_after, two, n_parts, ids, counts, *refs):
    refs = list(refs)

    def take(n):
        taken = refs[:n]
        del refs[:n]
        return taken

    pairs = [take(2 if two else 1) for _ in whiches]
    (weight,) = take(1)
    inits = take(n_init)
    bias = take(has_bias)
    take(n_after)
    outs = [take(n_parts) for _ in whiches]
    h_buf, w_buf, acc, sems = refs
    slots = ids.shape[2]
    per_shard = weight.shape[0] // BLK
    position = lax.axis_index("dp")
    edge = (position == 0) | (position == lax.axis_size("dp") - 1)

    def slab(k, s):
        block = lax.rem(ids[place(*whiches[k]), 0, s], per_shard)
        return pltpu.make_async_copy(
            weight.at[pl.ds(pl.multiple_of(block * BLK, BLK), BLK)],
            w_buf.at[k, pl.ds(s * BLK, BLK)],
            sems.at[k, s],
        )

    def fetch(k, source):
        return pltpu.make_async_copy(source, h_buf.at[k], sems.at[k, slots])

    for k, which in enumerate(whiches):
        if two:
            pl.when(edge)(lambda k=k: fetch(k, pairs[k][1]).start())
            pl.when(jnp.logical_not(edge))(lambda k=k: fetch(k, pairs[k][0]).start())
        else:
            fetch(k, pairs[k][0]).start()
        for s in range(slots):
            pl.when(s < counts[0, place(*which)])(lambda k=k, s=s: slab(k, s).start())
    for k in range(len(whiches)):
        if bias and whiches[k][0] == 0:
            acc[k] = jnp.broadcast_to(bias[0][...], acc.shape[1:])
        elif not inits:
            acc[k] = jnp.zeros(acc.shape[1:], jnp.float32)
    for at, init in enumerate(inits):
        acc[0, pl.ds(at * init.shape[0], init.shape[0]), :] = init[...].astype(jnp.float32)
    for k, which in enumerate(whiches):
        count = counts[0, place(*which)]
        fetch(k, pairs[k][0]).wait()
        for s in range(0, slots, 2):

            @pl.when(s < count)
            def _(k=k, s=s, count=count):
                slab(k, s).wait()
                pl.when(s + 1 < count)(lambda: slab(k, s + 1).wait())

                @pl.when(s + 1 >= count)
                def _():
                    w_buf[k, pl.ds((s + 1) * BLK, BLK), :] = jnp.zeros((BLK, w_buf.shape[2]), w_buf.dtype)

                acc[k] += jnp.dot(
                    h_buf[k, :, pl.ds(s * BLK, 2 * BLK)],
                    w_buf[k, pl.ds(s * BLK, 2 * BLK), :],
                    preferred_element_type=jnp.float32,
                )

        for at, out in enumerate(outs[k]):
            out[...] = acc[k, pl.ds(at * out.shape[0], out.shape[0]), :].astype(out.dtype)


def down(whiches, ids, counts, pairs, weight, inits=(), bias=None, after=(), dtypes=(jnp.bfloat16,), parts=1):
    slots = ids.shape[2]
    width = weight.shape[1]
    count = len(whiches)
    two = len(pairs[0]) == 2
    extra = list(inits) + ([] if bias is None else [bias])
    out = pl.pallas_call(
        functools.partial(down_kernel, whiches, len(inits), bias is not None, len(after), two, parts),
        out_shape=[jax.ShapeDtypeStruct((BLK // parts, width), dtype) for dtype in dtypes for _ in range(parts)],
        in_specs=[SMEM, SMEM] + [ANY] * (count * len(pairs[0]) + 1) + [VMEM] * len(extra) + [ANY] * len(after),
        out_specs=[VMEM] * (parts * count),
        scratch_shapes=[
            pltpu.VMEM((count, BLK, slots * BLK), jnp.bfloat16),
            pltpu.VMEM((count, slots * BLK, width), jnp.bfloat16),
            pltpu.VMEM((count, BLK, width), jnp.float32),
            pltpu.SemaphoreType.DMA((count, slots + 1)),
        ],
        compiler_params=pltpu.CompilerParams(vmem_limit_bytes=VMEM_LIMIT),
        cost_estimate=pl.CostEstimate(flops=COST, bytes_accessed=COST, transcendentals=0),
        name="down",
    )(ids, counts, *[x for pair in pairs for x in pair], weight, *extra, *after)
    return [out[k * parts : (k + 1) * parts] for k in range(count)]


def active(total, bias):
    return jnp.maximum(total + bias, 0.0).astype(jnp.bfloat16)


def small(body, name, outs, operands, after):
    def run(*refs):
        body(*refs[: len(operands)], *refs[len(operands) + len(after) :])

    return pl.pallas_call(
        run,
        out_shape=outs,
        in_specs=[VMEM] * len(operands) + [ANY] * len(after),
        out_specs=jax.tree.map(lambda _: VMEM, outs),
        compiler_params=pltpu.CompilerParams(vmem_limit_bytes=VMEM_LIMIT),
        cost_estimate=pl.CostEstimate(flops=COST, bytes_accessed=COST, transcendentals=0),
        name=name,
    )(*operands, *after)


def fold(part, got, after):
    def body(part, got, out):
        out[...] = (part[...].astype(jnp.float32) + got[...].astype(jnp.float32)).astype(out.dtype)

    return small(body, "fold", jax.ShapeDtypeStruct(part.shape, part.dtype), [part, got], after)


def mix(i, folded, other, table, part, after):
    shape = jax.ShapeDtypeStruct(folded.shape, folded.dtype)

    def body(folded, other, table, *refs):
        total = folded[...].astype(jnp.float32) + other[...].astype(jnp.float32)
        value = active(total, table[i : i + 1, :])
        refs[-1][...] = value
        if part is not None:
            position = lax.axis_index("dp")
            edge = (position == 0) | (position == lax.axis_size("dp") - 1)
            out = refs[1]

            @pl.when(edge)
            def _():
                out[...] = refs[0][...]

            @pl.when(jnp.logical_not(edge))
            def _():
                out[...] = value

    if part is None:
        value = small(body, "mix", shape, [folded, other, table], after)
        return value, value
    sent, value = small(body, "mix", [shape, shape], [folded, other, table, part], after)
    return value, sent


def plain(rows_in, up_weight, up_bias, down_weight, down_bias, active_ids, active_counts):
    gathered = lax.all_gather(rows_in, "tensor", axis=0, tiled=True)
    order = [(None, b, 1) for b in range(gathered.shape[0] // BLK)]
    table = bias_table(order, active_ids, active_counts, up_bias.reshape(-1, BLK))
    terms = []
    for b, which in enumerate(order):
        (part,) = up([which], active_ids, active_counts, [[gathered[b * BLK : (b + 1) * BLK]]], up_weight)
        summed = lax.psum(part, "dp").astype(jnp.float32)
        hidden = active(summed, table[b : b + 1])
        terms.append(down([which], active_ids, active_counts, [[hidden]], down_weight)[0][0])
    terms = jnp.concatenate(terms, axis=0)
    owned = lax.psum_scatter(terms, "tensor", scatter_dimension=0, tiled=True).astype(jnp.float32)
    return owned + down_bias[None, :]


def staged(rows_in, up_weight, up_bias, down_weight, down_bias, active_ids, active_counts):
    f32 = jnp.float32
    order = [(f, j, 2) for f, j in ((0, 0), (1, 0), (0, 1), (3, 0), (2, 0), (3, 1), (2, 1), (1, 1))]
    steps = len(order)
    lag = 3

    def swap(parts, flip):
        return [lax.ppermute(part, "tensor", [(t, t ^ flip) for t in range(4)]) for part in parts]

    first, low, high, table = head(
        order, active_ids, active_counts, rows_in, up_weight, up_bias.reshape(-1, BLK)
    )
    mine = [[low], [high]]
    across = [swap(block, 3) for block in mine]
    beside = [swap(block, 1) for block in mine]
    relayed = {}
    source = {0: mine, 1: beside, 2: relayed, 3: across}
    partial, folded, other, hidden, got, terms, near, far, own = {0: first}, {}, {}, {}, {}, {}, {}, {}, {}
    after = first
    line = []

    def do_up(some, after, keep=0):
        rows = [source[order[i][0]][order[i][1]] for i in some]
        out = up([order[i] for i in some], active_ids, active_counts, rows, up_weight, [after], keep)
        partial.update(zip(some, out))
        return out[len(some) :]

    def do_down(some, after, **more):
        pairs = [(hidden[i], got[i + lag]) for i in some]
        return down([order[i] for i in some], active_ids, active_counts, pairs, down_weight, after=after, **more)

    ups = {0: [(1, 2)], 2: [(3,)], 3: [(4,)], 4: [(5,)], 5: [(6,)], 6: [(7,)]}
    downs = {7: [(3,)], 8: [(4,)], 9: [(5,)], 10: [(6,)], 11: [(7,), (0, 1, 2)]}
    for i in range(steps + lag + 1):
        back = i - lag
        latest = after
        if i < steps + lag:
            sent = partial.get(i)
            if back >= 0:
                hidden[back], sent = mix(back, folded[back], other[back], table, partial.get(i), [])
                latest = sent
            got[i] = lax.ppermute(sent, "dp", [(0, 1), (1, 0), (2, 3), (3, 2)])
        for some in ups.get(i, ()):
            flip, j, _ = order[some[0]]
            rows = do_up(some, partial[some[0] - 1], 2 if flip == 3 else 0)
            latest = partial[some[0]]
            if flip == 3:
                relayed[j] = swap(rows, 1)
        if 0 <= i - 1 < steps:
            latest = folded[i - 1] = fold(partial[i - 1], got[i - 1], [])
            other[i - 1] = lax.ppermute(latest, "dp", [(1, 2), (2, 1)])
        for some in downs.get(i, ()):
            flip, j, _ = order[some[0]]
            if flip == 0:
                dtypes = [f32 if order[k][0] == 0 else jnp.bfloat16 for k in some]
                out = do_down(some, [latest] + line + far[0], bias=down_bias[None, :], dtypes=dtypes)
                for k, value in zip(some, out):
                    flip, j, _ = order[k]
                    if flip == 0:
                        own[j] = value[0]
                    else:
                        near[j] = swap(value, 1)
                latest = out[0][0]
                line = [latest]
                continue
            (out,) = do_down(some, [latest] + line, inits=terms[j] if flip == 2 else (), parts=1 if (flip, j) == (2, 0) else 2)
            latest = out[0]
            line = [latest]
            {1: near, 2: far, 3: terms}[flip][j] = swap(out, 2 if flip == 2 else 1)
        after = latest

    def joined(parts):
        return jnp.concatenate(parts, axis=0).astype(f32)

    return jnp.concatenate([own[j] + joined(near[j]) + joined(far[j]) for j in range(2)], axis=0)


def solution(mesh):
    placed = (
        P(("parts", "tensor"), "dp"),
        P("dp", "tensor"),
        P("tensor"),
        P("tensor", "dp"),
        P("dp"),
        P("parts", "tensor", None),
        P("parts", "tensor"),
    )

    def run(rows_in, up_weight, up_bias, down_weight, down_bias, active_ids, active_counts):
        rest = (up_weight, up_bias, down_weight, down_bias, active_ids, active_counts.T)
        if mesh.shape["tensor"] == 4 and mesh.shape["dp"] == 4 and rows_in.shape[0] == 2 * BLK:
            return staged(rows_in, *rest)
        return plain(rows_in, *rest)

    return jax.shard_map(
        run, mesh=mesh, in_specs=placed, out_specs=P(("parts", "tensor"), "dp"), check_vma=False
    )
```

```python
import functools

import jax
import jax.numpy as jnp
from jax import lax
from jax.experimental import pallas as pl
from jax.experimental.pallas import tpu as pltpu
from jax.sharding import PartitionSpec as P

BLK = 128
ANY = pl.BlockSpec(memory_space=pl.ANY)
SMEM = pl.BlockSpec(memory_space=pltpu.SMEM)
VMEM = pl.BlockSpec(memory_space=pltpu.VMEM)
MIB = 1024 * 1024
COST = 1
VMEM_LIMIT = 36 * MIB


def place(flip, step, per_owner):
    if flip is None:
        return step
    return (lax.axis_index("tensor") ^ flip) * per_owner + step


def projection(b, ids, counts, weight, x_buf, out, w_buf, sem):
    slots = ids.shape[2]
    per_shard = weight.shape[1] // BLK
    count = counts[0, b]

    def slab(s):
        block = lax.rem(ids[b, 0, s], per_shard)
        return pltpu.make_async_copy(
            weight.at[:, pl.ds(pl.multiple_of(block * BLK, BLK), BLK)],
            w_buf.at[:, pl.ds(s * BLK, BLK)],
            sem(s),
        )

    def start():
        for s in range(slots):
            pl.when(s < count)(lambda s=s: slab(s).start())

    def finish():
        for s in range(0, slots, 2):
            span = pl.ds(s * BLK, 2 * BLK)

            @pl.when(s < count)
            def _(s=s, span=span):
                slab(s).wait()
                pl.when(s + 1 < count)(lambda: slab(s + 1).wait())
                value = jnp.dot(x_buf[...], w_buf[:, span], preferred_element_type=jnp.float32)
                column = lax.broadcasted_iota(jnp.int32, value.shape, 1)
                live = (column < BLK) | (s + 1 < count)
                out[:, span] = jnp.where(live, value, 0.0).astype(out.dtype)

            @pl.when(s >= count)
            def _(span=span):
                out[:, span] = jnp.zeros((BLK, 2 * BLK), out.dtype)

    return start, finish


def fill_table(order, ids, counts, bias, out):
    slots = ids.shape[2]
    per_shard = bias.shape[0]
    for c, which in enumerate(order):
        b = place(*which)
        for s in range(slots):
            row = bias[pl.ds(lax.rem(ids[b, 0, s], per_shard), 1), :]
            out[pl.ds(c, 1), pl.ds(s * BLK, BLK)] = jnp.where(s < counts[0, b], row, 0.0)


def head_kernel(order, ids, counts, rows, weight, bias, out, low, high, table, w_buf, sems):
    slots = ids.shape[2]
    halves = [
        pltpu.make_async_copy(rows.at[pl.ds(j * BLK, BLK)], half, sems.at[slots + j])
        for j, half in enumerate((low, high))
    ]

    start, finish = projection(
        place(*order[0]), ids, counts, weight, low, out, w_buf, lambda s: sems.at[s]
    )
    for half in halves:
        half.start()
    start()
    fill_table(order, ids, counts, bias, table)
    for half in halves:
        half.wait()
    finish()


def head(order, ids, counts, rows, weight, bias):
    slots = ids.shape[2]
    width = weight.shape[0]
    return pl.pallas_call(
        functools.partial(head_kernel, order),
        out_shape=[
            jax.ShapeDtypeStruct((BLK, slots * BLK), jnp.bfloat16),
            jax.ShapeDtypeStruct((BLK, width), jnp.bfloat16),
            jax.ShapeDtypeStruct((BLK, width), jnp.bfloat16),
            jax.ShapeDtypeStruct((len(order), slots * BLK), jnp.float32),
        ],
        in_specs=[SMEM, SMEM, ANY, ANY, VMEM],
        out_specs=[VMEM] * 4,
        scratch_shapes=[
            pltpu.VMEM((width, slots * BLK), jnp.bfloat16),
            pltpu.SemaphoreType.DMA((slots + 2,)),
        ],
        compiler_params=pltpu.CompilerParams(vmem_limit_bytes=62 * MIB),
        cost_estimate=pl.CostEstimate(flops=COST, bytes_accessed=COST, transcendentals=0),
        name="head",
    )(ids, counts, rows, weight, bias)


def up_kernel(blocks, n_after, n_keep, ids, counts, weight, *refs):
    n_rows = [n for _, n in blocks]
    rows, refs = refs[: sum(n_rows)], refs[sum(n_rows) + n_after :]
    outs, kept = refs[: len(blocks)], refs[len(blocks) : len(blocks) + n_keep]
    x_buf, w_buf, sems, row_sems = refs[len(blocks) + n_keep :]
    fetches, steps = [], []
    for k, (which, n) in enumerate(blocks):
        height = BLK // n
        for part in range(n):
            at = len(fetches)
            fetches.append(
                pltpu.make_async_copy(
                    rows[at], x_buf.at[k, pl.ds(part * height, height)], row_sems.at[at]
                )
            )
        steps.append(
            projection(
                place(*which),
                ids,
                counts,
                weight,
                x_buf.at[k],
                outs[k],
                w_buf.at[k],
                lambda s, k=k: sems.at[k, s],
            )
        )
    for fetch in fetches:
        fetch.start()
    for start, _ in steps:
        start()
    for fetch in fetches:
        fetch.wait()
    for k, part in enumerate(kept):
        part[...] = x_buf[0, pl.ds(k * part.shape[0], part.shape[0]), :]
    for _, finish in steps:
        finish()


def up(whiches, ids, counts, rows, weight, after=(), keep=0):
    slots = ids.shape[2]
    width = weight.shape[0]
    count = len(whiches)
    parts = [part for block in rows for part in block]
    return pl.pallas_call(
        functools.partial(up_kernel, [(w, len(r)) for w, r in zip(whiches, rows)], len(after), keep),
        out_shape=[jax.ShapeDtypeStruct((BLK, slots * BLK), jnp.bfloat16)] * count
        + [jax.ShapeDtypeStruct((BLK // max(keep, 1), width), jnp.bfloat16)] * keep,
        in_specs=[SMEM, SMEM] + [ANY] * (1 + len(parts) + len(after)),
        out_specs=[VMEM] * (count + keep),
        scratch_shapes=[
            pltpu.VMEM((count, BLK, width), jnp.bfloat16),
            pltpu.VMEM((count, width, slots * BLK), jnp.bfloat16),
            pltpu.SemaphoreType.DMA((count, slots)),
            pltpu.SemaphoreType.DMA((len(parts),)),
        ],
        compiler_params=pltpu.CompilerParams(vmem_limit_bytes=VMEM_LIMIT),
        cost_estimate=pl.CostEstimate(flops=COST, bytes_accessed=COST, transcendentals=0),
        name="up",
    )(ids, counts, weight, *parts, *after)


def bias_table(order, ids, counts, bias):
    slots = ids.shape[2]
    return pl.pallas_call(
        functools.partial(fill_table, order),
        out_shape=jax.ShapeDtypeStruct((len(order), slots * BLK), jnp.float32),
        in_specs=[SMEM, SMEM, VMEM],
        out_specs=VMEM,
        compiler_params=pltpu.CompilerParams(vmem_limit_bytes=MIB),
        cost_estimate=pl.CostEstimate(flops=COST, bytes_accessed=COST, transcendentals=0),
        name="bias_table",
    )(ids, counts, bias)


def down_kernel(whiches, n_init, has_bias, n_after, two, n_parts, ids, counts, *refs):
    refs = list(refs)

    def take(n):
        taken = refs[:n]
        del refs[:n]
        return taken

    pairs = [take(2 if two else 1) for _ in whiches]
    (weight,) = take(1)
    inits = take(n_init)
    bias = take(has_bias)
    take(n_after)
    outs = [take(n_parts) for _ in whiches]
    h_buf, w_buf, acc, sems = refs
    slots = ids.shape[2]
    per_shard = weight.shape[0] // BLK
    position = lax.axis_index("dp")
    edge = (position == 0) | (position == lax.axis_size("dp") - 1)

    def slab(k, s):
        block = lax.rem(ids[place(*whiches[k]), 0, s], per_shard)
        return pltpu.make_async_copy(
            weight.at[pl.ds(pl.multiple_of(block * BLK, BLK), BLK)],
            w_buf.at[k, pl.ds(s * BLK, BLK)],
            sems.at[k, s],
        )

    def fetch(k, source):
        return pltpu.make_async_copy(source, h_buf.at[k], sems.at[k, slots])

    for k, which in enumerate(whiches):
        if two:
            pl.when(edge)(lambda k=k: fetch(k, pairs[k][1]).start())
            pl.when(jnp.logical_not(edge))(lambda k=k: fetch(k, pairs[k][0]).start())
        else:
            fetch(k, pairs[k][0]).start()
        for s in range(slots):
            pl.when(s < counts[0, place(*which)])(lambda k=k, s=s: slab(k, s).start())
    for k in range(len(whiches)):
        if bias and whiches[k][0] == 0:
            acc[k] = jnp.broadcast_to(bias[0][...], acc.shape[1:])
        elif not inits:
            acc[k] = jnp.zeros(acc.shape[1:], jnp.float32)
    for at, init in enumerate(inits):
        acc[0, pl.ds(at * init.shape[0], init.shape[0]), :] = init[...].astype(jnp.float32)
    for k, which in enumerate(whiches):
        count = counts[0, place(*which)]
        fetch(k, pairs[k][0]).wait()
        for s in range(0, slots, 2):

            @pl.when(s < count)
            def _(k=k, s=s, count=count):
                slab(k, s).wait()
                pl.when(s + 1 < count)(lambda: slab(k, s + 1).wait())

                @pl.when(s + 1 >= count)
                def _():
                    w_buf[k, pl.ds((s + 1) * BLK, BLK), :] = jnp.zeros((BLK, w_buf.shape[2]), w_buf.dtype)

                acc[k] += jnp.dot(
                    h_buf[k, :, pl.ds(s * BLK, 2 * BLK)],
                    w_buf[k, pl.ds(s * BLK, 2 * BLK), :],
                    preferred_element_type=jnp.float32,
                )

        for at, out in enumerate(outs[k]):
            out[...] = acc[k, pl.ds(at * out.shape[0], out.shape[0]), :].astype(out.dtype)


def down(whiches, ids, counts, pairs, weight, inits=(), bias=None, after=(), dtypes=(jnp.bfloat16,), parts=1):
    slots = ids.shape[2]
    width = weight.shape[1]
    count = len(whiches)
    two = len(pairs[0]) == 2
    extra = list(inits) + ([] if bias is None else [bias])
    out = pl.pallas_call(
        functools.partial(down_kernel, whiches, len(inits), bias is not None, len(after), two, parts),
        out_shape=[jax.ShapeDtypeStruct((BLK // parts, width), dtype) for dtype in dtypes for _ in range(parts)],
        in_specs=[SMEM, SMEM] + [ANY] * (count * len(pairs[0]) + 1) + [VMEM] * len(extra) + [ANY] * len(after),
        out_specs=[VMEM] * (parts * count),
        scratch_shapes=[
            pltpu.VMEM((count, BLK, slots * BLK), jnp.bfloat16),
            pltpu.VMEM((count, slots * BLK, width), jnp.bfloat16),
            pltpu.VMEM((count, BLK, width), jnp.float32),
            pltpu.SemaphoreType.DMA((count, slots + 1)),
        ],
        compiler_params=pltpu.CompilerParams(vmem_limit_bytes=VMEM_LIMIT),
        cost_estimate=pl.CostEstimate(flops=COST, bytes_accessed=COST, transcendentals=0),
        name="down",
    )(ids, counts, *[x for pair in pairs for x in pair], weight, *extra, *after)
    return [out[k * parts : (k + 1) * parts] for k in range(count)]


def active(total, bias):
    return jnp.maximum(total + bias, 0.0).astype(jnp.bfloat16)


def small(body, name, outs, operands, after):
    def run(*refs):
        body(*refs[: len(operands)], *refs[len(operands) + len(after) :])

    return pl.pallas_call(
        run,
        out_shape=outs,
        in_specs=[VMEM] * len(operands) + [ANY] * len(after),
        out_specs=jax.tree.map(lambda _: VMEM, outs),
        compiler_params=pltpu.CompilerParams(vmem_limit_bytes=VMEM_LIMIT),
        cost_estimate=pl.CostEstimate(flops=COST, bytes_accessed=COST, transcendentals=0),
        name=name,
    )(*operands, *after)


def fold(part, got, after):
    def body(part, got, out):
        out[...] = (part[...].astype(jnp.float32) + got[...].astype(jnp.float32)).astype(out.dtype)

    return small(body, "fold", jax.ShapeDtypeStruct(part.shape, part.dtype), [part, got], after)


def mix(i, folded, other, table, part, after):
    shape = jax.ShapeDtypeStruct(folded.shape, folded.dtype)

    def body(folded, other, table, *refs):
        total = folded[...].astype(jnp.float32) + other[...].astype(jnp.float32)
        value = active(total, table[i : i + 1, :])
        refs[-1][...] = value
        if part is not None:
            position = lax.axis_index("dp")
            edge = (position == 0) | (position == lax.axis_size("dp") - 1)
            out = refs[1]

            @pl.when(edge)
            def _():
                out[...] = refs[0][...]

            @pl.when(jnp.logical_not(edge))
            def _():
                out[...] = value

    if part is None:
        value = small(body, "mix", shape, [folded, other, table], after)
        return value, value
    sent, value = small(body, "mix", [shape, shape], [folded, other, table, part], after)
    return value, sent


def plain(rows_in, up_weight, up_bias, down_weight, down_bias, active_ids, active_counts):
    gathered = lax.all_gather(rows_in, "tensor", axis=0, tiled=True)
    order = [(None, b, 1) for b in range(gathered.shape[0] // BLK)]
    table = bias_table(order, active_ids, active_counts, up_bias.reshape(-1, BLK))
    terms = []
    for b, which in enumerate(order):
        (part,) = up([which], active_ids, active_counts, [[gathered[b * BLK : (b + 1) * BLK]]], up_weight)
        summed = lax.psum(part, "dp").astype(jnp.float32)
        hidden = active(summed, table[b : b + 1])
        terms.append(down([which], active_ids, active_counts, [[hidden]], down_weight)[0][0])
    terms = jnp.concatenate(terms, axis=0)
    owned = lax.psum_scatter(terms, "tensor", scatter_dimension=0, tiled=True).astype(jnp.float32)
    return owned + down_bias[None, :]


def finish_kernel(counts, *refs):
    out, buf, sems = refs[-3:]
    copies = []
    for j, (n_near, n_far) in enumerate(counts):
        own, nears, fars = refs[0], refs[1 : 1 + n_near], refs[1 + n_near : 1 + n_near + n_far]
        refs = refs[1 + n_near + n_far :]
        buf[j] = own[...]
        for parts in (nears, fars):
            for at, part in enumerate(parts):
                buf[j, pl.ds(at * part.shape[0], part.shape[0]), :] += part[...].astype(jnp.float32)
        copies.append(pltpu.make_async_copy(buf.at[j], out.at[pl.ds(j * BLK, BLK)], sems.at[j]))
        copies[-1].start()
    for copy in copies:
        copy.wait()


def finish(own, near, far):
    operands = [x for j in range(2) for x in [own[j], *near[j], *far[j]]]
    width = own[0].shape[1]
    return pl.pallas_call(
        functools.partial(finish_kernel, [(len(near[j]), len(far[j])) for j in range(2)]),
        out_shape=jax.ShapeDtypeStruct((2 * BLK, width), jnp.float32),
        in_specs=[VMEM] * len(operands),
        out_specs=ANY,
        scratch_shapes=[pltpu.VMEM((2, BLK, width), jnp.float32), pltpu.SemaphoreType.DMA((2,))],
        compiler_params=pltpu.CompilerParams(vmem_limit_bytes=VMEM_LIMIT),
        cost_estimate=pl.CostEstimate(flops=COST, bytes_accessed=COST, transcendentals=0),
        name="finish",
    )(*operands)


def staged(rows_in, up_weight, up_bias, down_weight, down_bias, active_ids, active_counts):
    f32 = jnp.float32
    order = [(f, j, 2) for f, j in ((0, 0), (1, 0), (0, 1), (3, 0), (2, 0), (3, 1), (2, 1), (1, 1))]
    steps = len(order)
    lag = 3

    def swap(parts, flip):
        return [lax.ppermute(part, "tensor", [(t, t ^ flip) for t in range(4)]) for part in parts]

    first, low, high, table = head(
        order, active_ids, active_counts, rows_in, up_weight, up_bias.reshape(-1, BLK)
    )
    mine = [[low], [high]]
    across = [swap(block, 3) for block in mine]
    beside = [swap(block, 1) for block in mine]
    relayed = {}
    source = {0: mine, 1: beside, 2: relayed, 3: across}
    partial, folded, other, hidden, got, terms, near, far, own = {0: first}, {}, {}, {}, {}, {}, {}, {}, {}
    after = first
    line = []

    def do_up(some, after, keep=0):
        rows = [source[order[i][0]][order[i][1]] for i in some]
        out = up([order[i] for i in some], active_ids, active_counts, rows, up_weight, [after], keep)
        partial.update(zip(some, out))
        return out[len(some) :]

    def do_down(some, after, **more):
        pairs = [(hidden[i], got[i + lag]) for i in some]
        return down([order[i] for i in some], active_ids, active_counts, pairs, down_weight, after=after, **more)

    ups = {0: [(1, 2)], 2: [(3,)], 3: [(4,)], 4: [(5,)], 5: [(6,)], 6: [(7,)]}
    downs = {7: [(3,)], 8: [(4,)], 9: [(5,)], 10: [(6,)], 11: [(7,), (0, 1, 2)]}
    for i in range(steps + lag + 1):
        back = i - lag
        latest = after
        if i < steps + lag:
            sent = partial.get(i)
            if back >= 0:
                hidden[back], sent = mix(back, folded[back], other[back], table, partial.get(i), [])
                latest = sent
            got[i] = lax.ppermute(sent, "dp", [(0, 1), (1, 0), (2, 3), (3, 2)])
        for some in ups.get(i, ()):
            flip, j, _ = order[some[0]]
            rows = do_up(some, partial[some[0] - 1], 2 if flip == 3 else 0)
            latest = partial[some[0]]
            if flip == 3:
                relayed[j] = swap(rows, 1)
        if 0 <= i - 1 < steps:
            latest = folded[i - 1] = fold(partial[i - 1], got[i - 1], [])
            other[i - 1] = lax.ppermute(latest, "dp", [(1, 2), (2, 1)])
        for some in downs.get(i, ()):
            flip, j, _ = order[some[0]]
            if flip == 0:
                dtypes = [f32 if order[k][0] == 0 else jnp.bfloat16 for k in some]
                out = do_down(some, [latest] + line + far[0], bias=down_bias[None, :], dtypes=dtypes)
                for k, value in zip(some, out):
                    flip, j, _ = order[k]
                    if flip == 0:
                        own[j] = value[0]
                    else:
                        near[j] = swap(value, 1)
                latest = out[0][0]
                line = [latest]
                continue
            (out,) = do_down(some, [latest] + line, inits=terms[j] if flip == 2 else (), parts=1 if (flip, j) == (2, 0) else 2)
            latest = out[0]
            line = [latest]
            {1: near, 2: far, 3: terms}[flip][j] = swap(out, 2 if flip == 2 else 1)
        after = latest

    return finish(own, near, far)


def solution(mesh):
    placed = (
        P(("parts", "tensor"), "dp"),
        P("dp", "tensor"),
        P("tensor"),
        P("tensor", "dp"),
        P("dp"),
        P("parts", "tensor", None),
        P("parts", "tensor"),
    )

    def run(rows_in, up_weight, up_bias, down_weight, down_bias, active_ids, active_counts):
        rest = (up_weight, up_bias, down_weight, down_bias, active_ids, active_counts.T)
        if mesh.shape["tensor"] == 4 and mesh.shape["dp"] == 4 and rows_in.shape[0] == 2 * BLK:
            return staged(rows_in, *rest)
        return plain(rows_in, *rest)

    return jax.shard_map(
        run, mesh=mesh, in_specs=placed, out_specs=P(("parts", "tensor"), "dp"), check_vma=False
    )
```
